256 devices in a mesh: blk: 32 (over z, x_lo, core), head: 8 (over x_hi, y).
Axes of the slice: x: 4 (x_hi: 2, x_lo: 2; x = x_hi * 2 + x_lo), y: 4, z: 8, core: 2. Of those that a mesh axis runs over, the one named last changes fastest.
Arguments:
- queries: bfloat16 [131072, 512], P(('blk', 'head')), may hold values from -6 to 6
- keys: bfloat16 [131072, 512], P(('blk', 'head')), may hold values from -6 to 6
- values: bfloat16 [131072, 512], P(('blk', 'head')), may hold values from -6 to 6
- w_out: bfloat16 [512, 512], replicated, may hold values from -3 to 3
Outputs:
- projected: bfloat16 [131072, 512], P(('blk', 'head'))
The draws below stay inside these ranges and needn't reach their ends.
All inputs are finite; a program needn't handle non-finite values.
Results may differ from the reference program's by a relative error of at most 0.0054.
Values may be sent and summed in bfloat16 or wider, within the bound.
A program may use at most 128 MiB of HBM per device.

```python
import jax
import jax.numpy as jnp
from jax import lax

D = 512
HEADS = 8
HEAD_DIM = 64
TOK_DEV = 512
TOKENS = 131072
N_BLK = 32
N_HEAD = 8


def draw_queries(key, part):
    key = jax.random.fold_in(key, 11)
    base = jnp.clip(1.4 * jax.random.normal(key, (TOKENS, D), jnp.float32), -6.0, 6.0)
    return base.astype(jnp.bfloat16)


def draw_keys(key, part):
    key = jax.random.fold_in(key, 23)
    base = jnp.clip(1.4 * jax.random.normal(key, (TOKENS, D), jnp.float32), -6.0, 6.0)
    return base.astype(jnp.bfloat16)


def block_scale(stream_key, dims, pieces, smallest, top_value):
    def one(dim, shards_of):
        heights = jax.random.uniform(jax.random.fold_in(jax.random.fold_in(stream_key, 6), dim), (shards_of,), jnp.float32, smallest / len(pieces), top_value / len(pieces))
        return jnp.repeat(jnp.exp(heights), dims[dim] // shards_of).reshape((-1,) + (1,) * (len(dims) - dim - 1))

    loudness = one(*pieces[0])
    for cut in pieces[1:]:
        loudness = loudness * one(*cut)
    return loudness


def centred(own_key, extent, scale, most, cuts=(), dtype=jnp.bfloat16):
    values = jax.random.normal(own_key, extent, jnp.float32) * scale
    if len(cuts) > 0:
        values = block_scale(own_key, extent, cuts, -0.22, 0.18) * values
    return jnp.clip(values, min=-most, max=most).astype(dtype)


def setup_inputs(seed: int = 0) -> dict:
    streams_of = jax.random.split(jax.random.key(seed), 5)
    return {
        "queries": draw_queries(jax.random.fold_in(streams_of[4], 71), 0),
        "keys": draw_keys(jax.random.fold_in(streams_of[4], 71), 0),
        "values": centred(streams_of[2], (TOKENS, D), 1.0, 6.0, ((0, 256),)),
        "w_out": centred(streams_of[3], (D, D), 0.5, 3.0),
    }


scaling = 0.125


def attend(queries, keys, values):
    rows, heads, size = queries.shape
    step = 512 if rows % 512 == 0 else rows
    q_heads = jnp.transpose(queries, (1, 0, 2)).reshape(heads, rows // step, step, size)
    k_heads = jnp.transpose(keys, (1, 0, 2))
    v_heads = jnp.transpose(values, (1, 0, 2))

    def per_head(items):
        q_one, k_one, v_one = items

        def per_block(q_block):
            scores = jnp.dot(q_block, k_one.T, preferred_element_type=jnp.float32) * scaling
            top = jnp.max(scores, axis=1, keepdims=True)
            expo = jnp.exp(scores - top)
            total = jnp.sum(expo, axis=1, keepdims=True)
            probs = expo.astype(jnp.bfloat16)
            mixed = jnp.dot(probs, v_one, preferred_element_type=jnp.float32) / total
            return mixed.astype(jnp.bfloat16)

        return lax.map(per_block, q_one)

    result = lax.map(per_head, (q_heads, k_heads, v_heads))
    return jnp.transpose(result.reshape(heads, rows, size), (1, 0, 2))


def reference(queries, keys, values, w_out):
    block = TOK_DEV * N_HEAD
    q_four = queries.reshape(N_BLK, block, HEADS, HEAD_DIM)
    k_four = keys.reshape(N_BLK, block, HEADS, HEAD_DIM)
    v_four = values.reshape(N_BLK, block, HEADS, HEAD_DIM)
    k_next = jnp.roll(k_four, -1, axis=0)
    v_next = jnp.roll(v_four, -1, axis=0)

    def per_blk(items):
        q_one, k_one, k_two, v_one, v_two = items
        return attend(q_one, jnp.concatenate([k_one, k_two], axis=0), jnp.concatenate([v_one, v_two], axis=0))

    mixed = lax.map(per_blk, (q_four, k_four, k_next, v_four, v_next))
    mixed = mixed.reshape(N_BLK * block, HEADS * HEAD_DIM)
    return jnp.dot(mixed, w_out, preferred_element_type=jnp.float32).astype(jnp.bfloat16)
```

```python
import jax
import jax.numpy as jnp
from jax import lax
from jax.experimental import pallas as pl
from jax.experimental.pallas import tpu as pltpu
from jax.sharding import PartitionSpec as P

HEADS = 8
HEAD_DIM = 64
TOK = 512
N_BLK = 32
WIDE = HEADS * HEAD_DIM
VROWS = 80
SUB = 256
GROUP = 4
TILE = GROUP * TOK
SCALE = 0.125 * 1.4426950408889634
F32 = jnp.float32
BF16 = jnp.bfloat16
MESH = pl.DeviceIdType.MESH
Y_FIRST = (1, 3, 2, 4, 5, 7, 6)


def mirror(r):
    if isinstance(r, int):
        return (r // 4) * 4 + (4 - r % 4) % 4
    return lax.div(r, 4) * 4 + lax.rem(4 - lax.rem(r, 4), 4)


def kernel(
    q_ref, k_ref, v_ref, w_ref, out_ref,
    q_send, k_send, v_send, q_in, k_in, v_in, q_wide, k_wide,
    acc, top, s_even, s_odd, o_send, o_in,
    q_ss, q_rs, k_ss, k_rs, v_ss, v_rs, o_ss, o_rs,
):
    blk = lax.axis_index("blk")
    head = lax.axis_index("head")
    before = lax.rem(blk + N_BLK - 1, N_BLK)
    behind = lax.rem(blk + 1, N_BLK)

    def peer(r):
        far = lax.rem(head // 4 + r // 4, 2)
        near = lax.rem(lax.rem(head, 4) + lax.rem(r, 4), 4)
        return far * 4 + near

    barrier = pltpu.get_barrier_semaphore()
    for r in Y_FIRST:
        pl.semaphore_signal(barrier, inc=1, device_id=(blk, peer(r)), device_id_type=MESH)
    pl.semaphore_signal(barrier, inc=1, device_id=(behind, head), device_id_type=MESH)

    def send_q(r):
        p, s = peer(r), mirror(r)
        return pltpu.make_async_remote_copy(
            src_ref=q_send.at[p], dst_ref=q_in.at[s], send_sem=q_ss.at[r], recv_sem=q_rs.at[s],
            device_id=(blk, p), device_id_type=MESH)

    def send_k(r):
        p, s = peer(r), mirror(r)
        return pltpu.make_async_remote_copy(
            src_ref=k_send.at[p], dst_ref=k_in.at[s], send_sem=k_ss.at[r], recv_sem=k_rs.at[s],
            device_id=(blk, p), device_id_type=MESH)

    def send_v(r):
        p, s = peer(r), mirror(r)
        return pltpu.make_async_remote_copy(
            src_ref=v_send.at[p], dst_ref=v_in.at[s, pl.ds(0, HEAD_DIM)],
            send_sem=v_ss.at[r], recv_sem=v_rs.at[s],
            device_id=(blk, p), device_id_type=MESH)

    def pass_k(r):
        return pltpu.make_async_remote_copy(
            src_ref=k_in.at[r], dst_ref=k_in.at[8 + r], send_sem=k_ss.at[8 + r],
            recv_sem=k_rs.at[8 + r], device_id=(before, head), device_id_type=MESH)

    def pass_v(r):
        return pltpu.make_async_remote_copy(
            src_ref=v_in.at[r, pl.ds(0, HEAD_DIM)], dst_ref=v_in.at[8 + r, pl.ds(0, HEAD_DIM)],
            send_sem=v_ss.at[8 + r], recv_sem=v_rs.at[8 + r],
            device_id=(before, head), device_id_type=MESH)

    def send_o(r):
        return pltpu.make_async_remote_copy(
            src_ref=o_send.at[r], dst_ref=o_in.at[head], send_sem=o_ss.at[r], recv_sem=o_rs.at[head],
            device_id=(blk, peer(r)), device_id_type=MESH)

    half = TOK // 2
    left = lax.broadcasted_iota(jnp.int32, (half, 128), 1) < HEAD_DIM

    def swap(x):
        return pltpu.roll(x, HEAD_DIM, 1)

    for pair in range(HEADS // 2):
        cols = slice(pair * 128, pair * 128 + 128)
        a = k_ref[0:half, cols].astype(F32)
        b = k_ref[half:TOK, cols].astype(F32)
        k_send[2 * pair] = jnp.where(left, a, swap(b)).astype(BF16)
        k_send[2 * pair + 1] = jnp.where(left, swap(a), b).astype(BF16)
    pl.semaphore_wait(barrier, 8)
    for r in (1, 3, 2):
        send_k(r).start()

    def transpose_into(src, dst):
        for pair in range(HEADS // 2):
            t = src[:, pair * 128:pair * 128 + 128].T
            dst[2 * pair] = t[:HEAD_DIM]
            dst[2 * pair + 1] = t[HEAD_DIM:]

    transpose_into(v_ref, v_send)
    for r in (1, 3, 2):
        send_v(r).start()
    transpose_into(q_ref, q_send)
    for r in Y_FIRST:
        send_q(r).start()
    for r in (4, 5, 7, 6):
        send_k(r).start()
        send_v(r).start()

    k_in[0] = k_send[head]
    v_in[0, 0:HEAD_DIM] = v_send[head]
    pass_k(0).start()
    pass_v(0).start()
    for s in range(16):
        v_in[s, HEAD_DIM:VROWS] = jnp.ones((VROWS - HEAD_DIM, TOK), BF16)

    def widen_q(q, s):
        scaled = q.astype(F32) * SCALE
        high = scaled.astype(BF16)
        q_wide[s, 0:HEAD_DIM] = high
        q_wide[s, HEAD_DIM:2 * HEAD_DIM] = (scaled - high.astype(F32)).astype(BF16)

    def widen_k(s):
        x = k_in[s].astype(F32)
        y = swap(x)
        k_wide[s, 0:half] = jnp.where(left, x, y).astype(BF16)
        k_wide[s, half:TOK] = jnp.where(left, y, x).astype(BF16)

    widen_q(q_send[head], 0)
    widen_k(0)
    acc[...] = jnp.zeros_like(acc)
    top[...] = jnp.full(top.shape, -1e30, F32)

    def arrive(r):
        send_k(mirror(r)).wait_recv()
        send_v(mirror(r)).wait_recv()
        pass_k(r).start()
        pass_v(r).start()
        widen_k(r)

    def arrive_next(r):
        pass_k(r).wait_recv()
        pass_v(r).wait_recv()
        widen_k(8 + r)

    for r in (1, 3, 2):
        arrive(r)

    def where(t):
        g = t // 8
        return lax.rem(t + g // 3, 8), g

    def scores(dst, t):
        i, g = where(t)
        q = q_wide[i]
        most = None
        for u in range(TILE // SUB):
            k = k_wide[g * GROUP + u // 2, (u % 2) * SUB:(u % 2 + 1) * SUB]
            s = jnp.dot(k, q, preferred_element_type=F32)
            dst[u * SUB:(u + 1) * SUB] = s
            m = jnp.max(s, axis=0, keepdims=True)
            most = m if most is None else jnp.maximum(most, m)
        return most

    def step(now, later, t, most):
        @pl.when(t < 7)
        def _():
            send_q(mirror(t + 1)).wait_recv()
            widen_q(q_in[t + 1], t + 1)

        @pl.when(t == 7)
        def _():
            for r in (4, 5, 7, 6):
                arrive(r)

        @pl.when(t == 15)
        def _():
            for r in range(4):
                arrive_next(r)

        @pl.when(t == 23)
        def _():
            for r in range(4, 8):
                arrive_next(r)

        i, g = where(t)
        old = top[i]
        new = jnp.maximum(old, most)
        top[i] = new
        i2, g2 = where(jnp.minimum(t + 1, 31))
        q = q_wide[i2]
        most = None
        mixed = None
        for u in range(TILE // SUB):
            rows = slice(u * SUB, (u + 1) * SUB)
            part = slice((u % 2) * SUB, (u % 2 + 1) * SUB)
            s = jnp.dot(k_wide[g2 * GROUP + u // 2, part], q, preferred_element_type=F32)
            later[rows] = s
            m = jnp.max(s, axis=0, keepdims=True)
            most = m if most is None else jnp.maximum(most, m)
            probs = jnp.exp2(now[rows] - new).astype(BF16)
            d = jnp.dot(v_in[g * GROUP + u // 2, :, part], probs, preferred_element_type=F32)
            mixed = d if mixed is None else mixed + d
        acc[i] = acc[i] * jnp.exp2(old - new) + mixed

        @pl.when(t >= 24)
        def _():
            a = acc[i]
            o = (a[0:HEAD_DIM] / a[HEAD_DIM:HEAD_DIM + 1]).astype(BF16)

            @pl.when(t < 31)
            def _():
                o_send[i] = o
                send_o(i).start()

            @pl.when(t == 31)
            def _():
                o_in[head] = o

        return most

    most = scores(s_even, 0)

    def two(n, most):
        most = step(s_even, s_odd, 2 * n, most)
        return step(s_odd, s_even, 2 * n + 1, most)

    lax.fori_loop(0, 16, two, most)

    for r in range(1, 8):
        p = peer(r)
        pltpu.make_async_remote_copy(
            src_ref=o_send.at[r], dst_ref=o_in.at[p], send_sem=o_ss.at[r], recv_sem=o_rs.at[p],
            device_id=(blk, p), device_id_type=MESH).wait_recv()
    mixed = o_in[...].reshape(WIDE, TOK)
    out_ref[...] = lax.dot_general(
        mixed, w_ref[...], (((0,), (0,)), ((), ())), preferred_element_type=F32
    ).astype(BF16)

    for r in range(1, 8):
        send_q(r).wait_send()
        send_k(r).wait_send()
        send_v(r).wait_send()
        send_o(r).wait_send()
    for r in range(8):
        pass_k(r).wait_send()
        pass_v(r).wait_send()


def on_device(queries, keys, values, w_out):
    vmem = pl.BlockSpec(memory_space=pltpu.VMEM)
    dma = pltpu.SemaphoreType.DMA
    return pl.pallas_call(
        kernel,
        out_shape=jax.ShapeDtypeStruct((TOK, WIDE), BF16),
        in_specs=[vmem] * 4,
        out_specs=vmem,
        scratch_shapes=[
            pltpu.VMEM((8, HEAD_DIM, TOK), BF16),
            pltpu.VMEM((8, TOK // 2, 128), BF16),
            pltpu.VMEM((8, HEAD_DIM, TOK), BF16),
            pltpu.VMEM((8, HEAD_DIM, TOK), BF16),
            pltpu.VMEM((16, TOK // 2, 128), BF16),
            pltpu.VMEM((16, VROWS, TOK), BF16),
            pltpu.VMEM((8, 2 * HEAD_DIM, TOK), BF16),
            pltpu.VMEM((16, TOK, 2 * HEAD_DIM), BF16),
            pltpu.VMEM((8, VROWS, TOK), F32),
            pltpu.VMEM((8, 1, TOK), F32),
            pltpu.VMEM((TILE, TOK), F32),
            pltpu.VMEM((TILE, TOK), F32),
            pltpu.VMEM((8, HEAD_DIM, TOK), BF16),
            pltpu.VMEM((8, HEAD_DIM, TOK), BF16),
            dma((8,)), dma((8,)), dma((16,)), dma((16,)),
            dma((16,)), dma((16,)), dma((8,)), dma((8,)),
        ],
        compiler_params=pltpu.CompilerParams(
            collective_id=0, has_side_effects=True, vmem_limit_bytes=48 * 2**20
        ),
        cost_estimate=pl.CostEstimate(
            flops=2 * 2 * TOK * WIDE * 16 * TOK + 2 * TOK * WIDE * WIDE,
            bytes_accessed=5 * TOK * WIDE * 2,
            transcendentals=TOK * HEADS * 16 * TOK,
        ),
    )(queries, keys, values, w_out)


def solution(mesh):
    split = P(("blk", "head"), None)
    return jax.shard_map(
        on_device, mesh=mesh, in_specs=(split, split, split, P()), out_specs=split, check_vma=False
    )
```

```python
import jax
import jax.numpy as jnp
from jax import lax
from jax.experimental import pallas as pl
from jax.experimental.pallas import tpu as pltpu
from jax.sharding import PartitionSpec as P

HEADS = 8
HEAD_DIM = 64
TOK = 512
N_BLK = 32
WIDE = HEADS * HEAD_DIM
VROWS = 80
SUB = 256
GROUP = 4
TILE = GROUP * TOK
SCALE = 0.125 * 1.4426950408889634
F32 = jnp.float32
BF16 = jnp.bfloat16
MESH = pl.DeviceIdType.MESH
FAR = (0, 0, 0, 1, 0, 1, 1, 1)
NEAR = (0, 1, 3, 0, 2, 1, 3, 2)
MIRROR = (0, 2, 1, 3, 4, 6, 5, 7)
SECOND = range(4, 8)


def kernel(
    q_hbm, k_hbm, v_hbm, w_hbm, out_ref,
    q_ref, k_ref, v_ref, w_ref, load,
    kv_send, q_send, kv_in, q_in, q_wide, k_wide, v_wide,
    acc, top, s_even, s_odd, o_send, o_in,
    kv_ss, kv_rs, q_ss, q_rs, pass_ss, pass_rs, o_ss, o_rs,
):
    loads = [
        pltpu.make_async_copy(hbm, ref, load.at[n])
        for n, (hbm, ref) in enumerate(
            ((k_hbm, k_ref), (v_hbm, v_ref), (q_hbm, q_ref), (w_hbm, w_ref)))
    ]
    for copy in loads:
        copy.start()

    blk = lax.axis_index("blk")
    head = lax.axis_index("head")
    before = lax.rem(blk + N_BLK - 1, N_BLK)
    behind = lax.rem(blk + 1, N_BLK)

    def peer(r):
        far = lax.rem(head // 4 + FAR[r], 2)
        near = lax.rem(lax.rem(head, 4) + NEAR[r], 4)
        return far * 4 + near

    barrier = pltpu.get_barrier_semaphore()
    for r in range(1, 8):
        pl.semaphore_signal(barrier, inc=1, device_id=(blk, peer(r)), device_id_type=MESH)
    pl.semaphore_signal(barrier, inc=1, device_id=(behind, head), device_id_type=MESH)

    def remote(src, dst, send, recv, device):
        return pltpu.make_async_remote_copy(
            src_ref=src, dst_ref=dst, send_sem=send, recv_sem=recv,
            device_id=device, device_id_type=MESH)

    def send_q(r):
        p, s = peer(r), MIRROR[r]
        return remote(q_send.at[p], q_in.at[s], q_ss.at[r], q_rs.at[s], (blk, p))

    def send_kv(r):
        p, s = peer(r), MIRROR[r]
        return remote(kv_send.at[p], kv_in.at[s], kv_ss.at[r], kv_rs.at[s], (blk, p))

    def pass_kv(n):
        return remote(
            kv_in.at[pl.ds(4 * n, 4)], kv_in.at[pl.ds(8 + 4 * n, 4)],
            pass_ss.at[n], pass_rs.at[n], (before, head))

    def send_o(r):
        p = peer(r)
        return remote(o_send.at[r], o_in.at[head], o_ss.at[r], o_rs.at[head], (blk, p))

    left = lax.broadcasted_iota(jnp.int32, (HEAD_DIM, 128), 1) < HEAD_DIM
    half = TOK // 2

    def swap(x):
        return pltpu.roll(x, HEAD_DIM, 1)

    def transpose_into(src, dst, at):
        for pair in range(HEADS // 2):
            t = src[:, pair * 128:pair * 128 + 128].T
            dst[2 * pair, at:at + HEAD_DIM] = t[:HEAD_DIM]
            dst[2 * pair + 1, at:at + HEAD_DIM] = t[HEAD_DIM:]

    loads[0].wait()
    for pair in range(HEADS // 2):
        cols = slice(pair * 128, pair * 128 + 128)
        for c in range(4):
            a = k_ref[c * 64:c * 64 + 64, cols].astype(F32)
            b = k_ref[half + c * 64:half + c * 64 + 64, cols].astype(F32)
            lanes = slice(c * 128, c * 128 + 128)
            kv_send[2 * pair, 0:HEAD_DIM, lanes] = jnp.where(left, a, swap(b)).astype(BF16)
            kv_send[2 * pair + 1, 0:HEAD_DIM, lanes] = jnp.where(left, swap(a), b).astype(BF16)
    loads[1].wait()
    transpose_into(v_ref, kv_send, HEAD_DIM)
    pl.semaphore_wait(barrier, 8)
    for r in (1, 2, 3):
        send_kv(r).start()
    loads[2].wait()
    transpose_into(q_ref, q_send, 0)
    for r in range(1, 8):
        send_q(r).start()

    def widen_q(q, s):
        scaled = q.astype(F32) * SCALE
        high = scaled.astype(BF16)
        q_wide[s, 0:HEAD_DIM] = high
        q_wide[s, HEAD_DIM:2 * HEAD_DIM] = (scaled - high.astype(F32)).astype(BF16)

    def widen_kv(s):
        for c in range(4):
            x = kv_in[s, 0:HEAD_DIM, c * 128:c * 128 + 128].astype(F32)
            y = swap(x)
            k_wide[s, c * 64:c * 64 + 64] = jnp.where(left, x, y).astype(BF16)
            k_wide[s, half + c * 64:half + c * 64 + 64] = jnp.where(left, y, x).astype(BF16)
        v_wide[s, 0:HEAD_DIM] = kv_in[s, HEAD_DIM:2 * HEAD_DIM]

    kv_in[0] = kv_send[head]
    for s in range(16):
        v_wide[s, HEAD_DIM:VROWS] = jnp.ones((VROWS - HEAD_DIM, TOK), BF16)
    acc[...] = jnp.zeros_like(acc)
    top[...] = jnp.full(top.shape, -1e30, F32)
    widen_q(q_send[head], 0)
    widen_kv(0)

    def arrive(n):
        for r in range(4 * n, 4 * n + 4):
            if r > 0:
                send_kv(MIRROR[r]).wait_recv()
                widen_kv(r)

    def arrive_next(n):
        pass_kv(n).wait_recv()
        for r in range(8 + 4 * n, 12 + 4 * n):
            widen_kv(r)

    arrive(0)
    for r in SECOND:
        send_kv(r).start()

    def where(t):
        second = t // 16
        u = t % 16
        c = u // 7
        up = (1 - c) * (2 - c) // 2
        down = c * (2 - c)
        own = c * (c - 1) // 2
        i = (1 - second) * (u % 8) + second * (up * (u + 1) + down * (14 - u))
        g = (1 - second) * (u // 8) + second * (2 * up + 3 * down + own * (u - 12))
        return i, g

    def tile(dst, t, src, t_src, new):
        i, g = where(t)
        q = q_wide[i]
        if src is not None:
            g_src = where(t_src)[1]
        most = mixed = None
        for u in range(TILE // SUB):
            rows = slice(u * SUB, (u + 1) * SUB)
            part = slice((u % 2) * SUB, (u % 2 + 1) * SUB)
            s = jnp.dot(k_wide[g * GROUP + u // 2, part], q, preferred_element_type=F32)
            dst[rows] = s
            m = jnp.max(s, axis=0, keepdims=True)
            most = m if most is None else jnp.maximum(most, m)
            if src is not None:
                probs = jnp.exp2(src[rows] - new).astype(BF16)
                d = jnp.dot(
                    v_wide[g_src * GROUP + u // 2, :, part], probs, preferred_element_type=F32)
                mixed = d if mixed is None else mixed + d
        return most, mixed

    def step(now, later, t, most):
        @pl.when(t < 7)
        def _():
            r = t + 1
            remote(q_send.at[r], q_in.at[r], q_ss.at[r], q_rs.at[r], (before, head)).wait_recv()
            widen_q(q_in[r], r)

        @pl.when(t == 7)
        def _():
            arrive(1)
            pass_kv(0).start()

        @pl.when(t == 11)
        def _():
            pass_kv(1).start()

        @pl.when(t == 15)
        def _():
            arrive_next(0)

        @pl.when(t == 22)
        def _():
            arrive_next(1)

        i = where(t)[0]
        old = top[i]
        new = jnp.maximum(old, most)
        top[i] = new
        most, mixed = tile(later, (t + 1) % 32, now, t, new)
        acc[i] = acc[i] * jnp.exp2(old - new) + mixed

        @pl.when(t >= 23)
        def _():
            a = acc[i]
            o_send[i] = (a[0:HEAD_DIM] / a[HEAD_DIM:HEAD_DIM + 1]).astype(BF16)

        for r in range(1, 8):
            @pl.when(t == 30 - r)
            def _():
                send_o(r).start()

        return most

    most, _ = tile(s_even, 0, None, 0, None)

    def two(n, most):
        most = step(s_even, s_odd, 2 * n, most)
        return step(s_odd, s_even, 2 * n + 1, most)

    lax.fori_loop(0, 16, two, most)

    o_in[head] = o_send[0]
    loads[3].wait()
    for r in range(1, 8):
        p = peer(r)
        remote(o_send.at[r], o_in.at[p], o_ss.at[r], o_rs.at[p], (blk, p)).wait_recv()
    mixed = o_in[...].reshape(WIDE, TOK)
    out_ref[...] = lax.dot_general(
        mixed, w_ref[...], (((0,), (0,)), ((), ())), preferred_element_type=F32
    ).astype(BF16)

    for r in range(1, 8):
        send_q(r).wait_send()
        send_kv(r).wait_send()
        send_o(r).wait_send()
    for n in range(2):
        pass_kv(n).wait_send()


def on_device(queries, keys, values, w_out):
    vmem = pl.BlockSpec(memory_space=pltpu.VMEM)
    hbm = pl.BlockSpec(memory_space=pltpu.HBM)
    dma = pltpu.SemaphoreType.DMA
    return pl.pallas_call(
        kernel,
        out_shape=jax.ShapeDtypeStruct((TOK, WIDE), BF16),
        in_specs=[hbm] * 4,
        out_specs=vmem,
        scratch_shapes=[
            *[pltpu.VMEM((TOK, WIDE), BF16)] * 4,
            dma((4,)),
            pltpu.VMEM((8, 2 * HEAD_DIM, TOK), BF16),
            pltpu.VMEM((8, HEAD_DIM, TOK), BF16),
            pltpu.VMEM((16, 2 * HEAD_DIM, TOK), BF16),
            pltpu.VMEM((8, HEAD_DIM, TOK), BF16),
            pltpu.VMEM((8, 2 * HEAD_DIM, TOK), BF16),
            pltpu.VMEM((16, TOK, 2 * HEAD_DIM), BF16),
            pltpu.VMEM((16, VROWS, TOK), BF16),
            pltpu.VMEM((8, VROWS, TOK), F32),
            pltpu.VMEM((8, 1, TOK), F32),
            pltpu.VMEM((TILE, TOK), F32),
            pltpu.VMEM((TILE, TOK), F32),
            pltpu.VMEM((8, HEAD_DIM, TOK), BF16),
            pltpu.VMEM((8, HEAD_DIM, TOK), BF16),
            dma((8,)), dma((8,)), dma((8,)), dma((8,)),
            dma((2,)), dma((2,)), dma((8,)), dma((8,)),
        ],
        compiler_params=pltpu.CompilerParams(
            collective_id=0, has_side_effects=True, vmem_limit_bytes=48 * 2**20
        ),
        cost_estimate=pl.CostEstimate(
            flops=2 * 2 * TOK * WIDE * 16 * TOK + 2 * TOK * WIDE * WIDE,
            bytes_accessed=5 * TOK * WIDE * 2,
            transcendentals=TOK * HEADS * 16 * TOK,
        ),
    )(queries, keys, values, w_out)


def solution(mesh):
    split = P(("blk", "head"), None)
    return jax.shard_map(
        on_device, mesh=mesh, in_specs=(split, split, split, P()), out_specs=split, check_vma=False
    )
```

```python
import jax
import jax.numpy as jnp
from jax import lax
from jax.experimental import pallas as pl
from jax.experimental.pallas import tpu as pltpu
from jax.sharding import PartitionSpec as P

HEADS = 8
HEAD_DIM = 64
TOK = 512
N_BLK = 32
WIDE = HEADS * HEAD_DIM
VROWS = 80
SUB = 256
GROUP = 4
TILE = GROUP * TOK
SCALE = 0.125 * 1.4426950408889634
F32 = jnp.float32
BF16 = jnp.bfloat16
MESH = pl.DeviceIdType.MESH
FAR = (0, 0, 0, 1, 0, 1, 1, 1)
NEAR = (0, 1, 3, 0, 2, 1, 3, 2)
MIRROR = (0, 2, 1, 3, 4, 6, 5, 7)
SECOND = range(4, 8)


def kernel(
    q_hbm, k_hbm, v_hbm, w_hbm, out_ref,
    q_ref, k_ref, v_ref, w_ref, load,
    kv_send, q_send, kv_in, q_in, q_wide, k_wide, v_wide,
    acc, top, s_even, s_odd, o_send, o_in,
    kv_ss, kv_rs, q_ss, q_rs, pass_ss, pass_rs, o_ss, o_rs,
):
    loads = [
        pltpu.make_async_copy(hbm, ref, load.at[n])
        for n, (hbm, ref) in enumerate(
            ((k_hbm, k_ref), (v_hbm, v_ref), (q_hbm, q_ref), (w_hbm, w_ref)))
    ]
    blk = lax.axis_index("blk")
    head = lax.axis_index("head")
    before = lax.rem(blk + N_BLK - 1, N_BLK)
    behind = lax.rem(blk + 1, N_BLK)

    x, y = lax.div(head, 4), lax.rem(head, 4)
    peers = [lax.rem(x + f, 2) * 4 + lax.rem(y + n, 4) for f, n in zip(FAR, NEAR)]

    def peer(r):
        return peers[r]

    for copy in loads[:2]:
        copy.start()
    barrier = pltpu.get_barrier_semaphore()
    for r in range(1, 8):
        pl.semaphore_signal(barrier, inc=1, device_id=(blk, peer(r)), device_id_type=MESH)
    pl.semaphore_signal(barrier, inc=1, device_id=(behind, head), device_id_type=MESH)
    for copy in loads[2:]:
        copy.start()

    def remote(src, dst, send, recv, device):
        return pltpu.make_async_remote_copy(
            src_ref=src, dst_ref=dst, send_sem=send, recv_sem=recv,
            device_id=device, device_id_type=MESH)

    def send_q(r):
        p, s = peer(r), MIRROR[r]
        return remote(q_send.at[p], q_in.at[s], q_ss.at[r], q_rs.at[s], (blk, p))

    def send_kv(r):
        p, s = peer(r), MIRROR[r]
        return remote(kv_send.at[p], kv_in.at[s], kv_ss.at[r], kv_rs.at[s], (blk, p))

    def pass_kv(n):
        return remote(
            kv_in.at[pl.ds(4 * n, 4)], kv_in.at[pl.ds(8 + 4 * n, 4)],
            pass_ss.at[n], pass_rs.at[n], (before, head))

    def send_o(r):
        p = peer(r)
        return remote(o_send.at[r], o_in.at[head], o_ss.at[r], o_rs.at[head], (blk, p))

    left = lax.broadcasted_iota(jnp.int32, (HEAD_DIM, 128), 1) < HEAD_DIM
    half = TOK // 2

    def swap(x):
        return pltpu.roll(x, HEAD_DIM, 1)

    def transpose_into(src, dst, at):
        for pair in range(HEADS // 2):
            t = src[:, pair * 128:pair * 128 + 128].T
            dst[2 * pair, at:at + HEAD_DIM] = t[:HEAD_DIM]
            dst[2 * pair + 1, at:at + HEAD_DIM] = t[HEAD_DIM:]

    loads[0].wait()
    for pair in range(HEADS // 2):
        cols = slice(pair * 128, pair * 128 + 128)
        for c in range(4):
            a = k_ref[c * 64:c * 64 + 64, cols].astype(F32)
            b = k_ref[half + c * 64:half + c * 64 + 64, cols].astype(F32)
            lanes = slice(c * 128, c * 128 + 128)
            kv_send[2 * pair, 0:HEAD_DIM, lanes] = jnp.where(left, a, swap(b)).astype(BF16)
            kv_send[2 * pair + 1, 0:HEAD_DIM, lanes] = jnp.where(left, swap(a), b).astype(BF16)
    loads[1].wait()
    transpose_into(v_ref, kv_send, HEAD_DIM)
    pl.semaphore_wait(barrier, 8)
    for r in (1, 2, 3):
        send_kv(r).start()
    loads[2].wait()
    transpose_into(q_ref, q_send, 0)
    for r in range(1, 8):
        send_q(r).start()

    def widen_q(q, s):
        scaled = q.astype(F32) * SCALE
        high = scaled.astype(BF16)
        q_wide[s, 0:HEAD_DIM] = high
        q_wide[s, HEAD_DIM:2 * HEAD_DIM] = (scaled - high.astype(F32)).astype(BF16)

    def widen_kv(s):
        for c in range(4):
            x = kv_in[s, 0:HEAD_DIM, c * 128:c * 128 + 128].astype(F32)
            y = swap(x)
            k_wide[s, c * 64:c * 64 + 64] = jnp.where(left, x, y).astype(BF16)
            k_wide[s, half + c * 64:half + c * 64 + 64] = jnp.where(left, y, x).astype(BF16)
        v_wide[s, 0:HEAD_DIM] = kv_in[s, HEAD_DIM:2 * HEAD_DIM]

    kv_in[0] = kv_send[head]
    for s in range(16):
        v_wide[s, HEAD_DIM:VROWS] = jnp.ones((VROWS - HEAD_DIM, TOK), BF16)
    acc[...] = jnp.zeros_like(acc)
    top[...] = jnp.full(top.shape, -1e30, F32)
    widen_q(q_send[head], 0)
    widen_kv(0)

    def arrive(n):
        for r in range(4 * n, 4 * n + 4):
            if r > 0:
                send_kv(MIRROR[r]).wait_recv()
                widen_kv(r)

    def arrive_next(n):
        pass_kv(n).wait_recv()
        for r in range(8 + 4 * n, 12 + 4 * n):
            widen_kv(r)

    arrive(0)

    pass_kv(0).start()

    def where(t):
        n = (t >= 8).astype(jnp.int32) + (t >= 15).astype(jnp.int32) + (t >= 22).astype(jnp.int32)
        i = jnp.where(t >= 29, 0, jnp.where(t >= 22, 29 - t, t - 7 * n))
        g = jnp.where(t >= 29, t - 28, n)
        return i, jnp.where(g == 1, 2, jnp.where(g == 2, 1, g))

    def tile(dst, t, src, t_src, new):
        i, g = where(t)
        q = q_wide[i]
        if src is not None:
            g_src = where(t_src)[1]
        most = mixed = None
        for u in range(TILE // SUB):
            rows = slice(u * SUB, (u + 1) * SUB)
            part = slice((u % 2) * SUB, (u % 2 + 1) * SUB)
            s = jnp.dot(k_wide[g * GROUP + u // 2, part], q, preferred_element_type=F32)
            dst[rows] = s
            m = jnp.max(s, axis=0, keepdims=True)
            most = m if most is None else jnp.maximum(most, m)
            if src is not None:
                probs = jnp.exp2(src[rows] - new).astype(BF16)
                d = jnp.dot(
                    v_wide[g_src * GROUP + u // 2, :, part], probs, preferred_element_type=F32)
                mixed = d if mixed is None else mixed + d
        return most, mixed

    def step(now, later, t, most):
        @pl.when(t < 7)
        def _():
            r = t + 1
            remote(q_send.at[r], q_in.at[r], q_ss.at[r], q_rs.at[r], (before, head)).wait_recv()
            widen_q(q_in[r], r)

        def at(when, act):
            @pl.when(t == when)
            def _():
                act()

        def rest():
            for r in SECOND:
                send_kv(r).start()

        def far_arrive():
            arrive(1)
            pass_kv(1).start()

        at(3, rest)
        at(7, lambda: arrive_next(0))
        at(12, far_arrive)
        at(21, lambda: arrive_next(1))

        i = where(t)[0]
        old = top[i]
        new = jnp.maximum(old, most)
        top[i] = new
        most, mixed = tile(later, jnp.minimum(t + 1, 31), now, t, new)
        acc[i] = acc[i] * jnp.exp2(old - new) + mixed

        @pl.when(t >= 22)
        def _():
            a = acc[i]
            o_send[i] = (a[0:HEAD_DIM] / a[HEAD_DIM:HEAD_DIM + 1]).astype(BF16)

        for r in range(1, 8):
            @pl.when(t == 29 - r)
            def _():
                send_o(r).start()

        return most

    most, _ = tile(s_even, jnp.int32(0), None, 0, None)

    def two(n, most):
        most = step(s_even, s_odd, 2 * n, most)
        return step(s_odd, s_even, 2 * n + 1, most)

    lax.fori_loop(0, 16, two, most)

    o_in[head] = o_send[0]
    loads[3].wait()
    for r in range(1, 8):
        p = peer(r)
        remote(o_send.at[r], o_in.at[p], o_ss.at[r], o_rs.at[p], (blk, p)).wait_recv()
    mixed = o_in[...].reshape(WIDE, TOK)
    out_ref[...] = lax.dot_general(
        mixed, w_ref[...], (((0,), (0,)), ((), ())), preferred_element_type=F32
    ).astype(BF16)

    for r in range(1, 8):
        send_q(r).wait_send()
        send_kv(r).wait_send()
        send_o(r).wait_send()
    for n in range(2):
        pass_kv(n).wait_send()


def on_device(queries, keys, values, w_out):
    vmem = pl.BlockSpec(memory_space=pltpu.VMEM)
    hbm = pl.BlockSpec(memory_space=pltpu.HBM)
    dma = pltpu.SemaphoreType.DMA
    return pl.pallas_call(
        kernel,
        out_shape=jax.ShapeDtypeStruct((TOK, WIDE), BF16),
        in_specs=[hbm] * 4,
        out_specs=vmem,
        scratch_shapes=[
            *[pltpu.VMEM((TOK, WIDE), BF16)] * 4,
            dma((4,)),
            pltpu.VMEM((8, 2 * HEAD_DIM, TOK), BF16),
            pltpu.VMEM((8, HEAD_DIM, TOK), BF16),
            pltpu.VMEM((16, 2 * HEAD_DIM, TOK), BF16),
            pltpu.VMEM((8, HEAD_DIM, TOK), BF16),
            pltpu.VMEM((8, 2 * HEAD_DIM, TOK), BF16),
            pltpu.VMEM((16, TOK, 2 * HEAD_DIM), BF16),
            pltpu.VMEM((16, VROWS, TOK), BF16),
            pltpu.VMEM((8, VROWS, TOK), F32),
            pltpu.VMEM((8, 1, TOK), F32),
            pltpu.VMEM((TILE, TOK), F32),
            pltpu.VMEM((TILE, TOK), F32),
            pltpu.VMEM((8, HEAD_DIM, TOK), BF16),
            pltpu.VMEM((8, HEAD_DIM, TOK), BF16),
            dma((8,)), dma((8,)), dma((8,)), dma((8,)),
            dma((2,)), dma((2,)), dma((8,)), dma((8,)),
        ],
        compiler_params=pltpu.CompilerParams(
            collective_id=0, has_side_effects=True, vmem_limit_bytes=48 * 2**20
        ),
        cost_estimate=pl.CostEstimate(
            flops=2 * 2 * TOK * WIDE * 16 * TOK + 2 * TOK * WIDE * WIDE,
            bytes_accessed=5 * TOK * WIDE * 2,
            transcendentals=TOK * HEADS * 16 * TOK,
        ),
    )(queries, keys, values, w_out)


def solution(mesh):
    split = P(("blk", "head"), None)
    return jax.shard_map(
        on_device, mesh=mesh, in_specs=(split, split, split, P()), out_specs=split, check_vma=False
    )
```

```python
import jax
import jax.numpy as jnp
from jax import lax
from jax.experimental import pallas as pl
from jax.experimental.pallas import tpu as pltpu
from jax.sharding import PartitionSpec as P

HEADS = 8
HEAD_DIM = 64
TOK = 512
N_BLK = 32
WIDE = HEADS * HEAD_DIM
VROWS = 80
SUB = 256
GROUP = 4
TILE = GROUP * TOK
SCALE = 0.125 * 1.4426950408889634
F32 = jnp.float32
BF16 = jnp.bfloat16
MESH = pl.DeviceIdType.MESH
FAR = (0, 0, 0, 1, 0, 1, 1, 1)
NEAR = (0, 1, 3, 0, 2, 1, 3, 2)
MIRROR = (0, 2, 1, 3, 4, 6, 5, 7)
SECOND = range(4, 8)


def kernel(
    q_hbm, k_hbm, v_hbm, w_hbm, out_ref,
    q_ref, k_ref, v_ref, w_ref, load,
    kv_send, q_send, kv_in, q_in, q_wide, k_wide, v_wide,
    acc, top, s_even, s_odd, o_send, o_in,
    kv_ss, kv_rs, q_ss, q_rs, pass_ss, pass_rs, o_ss, o_rs,
):
    loads = [
        pltpu.make_async_copy(hbm, ref, load.at[n])
        for n, (hbm, ref) in enumerate(
            ((k_hbm, k_ref), (v_hbm, v_ref), (q_hbm, q_ref), (w_hbm, w_ref)))
    ]
    blk = lax.axis_index("blk")
    head = lax.axis_index("head")
    before = lax.rem(blk + N_BLK - 1, N_BLK)
    behind = lax.rem(blk + 1, N_BLK)

    x, y = lax.div(head, 4), lax.rem(head, 4)
    peers = [lax.rem(x + f, 2) * 4 + lax.rem(y + n, 4) for f, n in zip(FAR, NEAR)]

    def peer(r):
        return peers[r]

    for copy in loads[:2]:
        copy.start()
    barrier = pltpu.get_barrier_semaphore()
    for r in range(1, 8):
        pl.semaphore_signal(barrier, inc=1, device_id=(blk, peer(r)), device_id_type=MESH)
    pl.semaphore_signal(barrier, inc=1, device_id=(behind, head), device_id_type=MESH)
    for copy in loads[2:]:
        copy.start()

    def remote(src, dst, send, recv, device):
        return pltpu.make_async_remote_copy(
            src_ref=src, dst_ref=dst, send_sem=send, recv_sem=recv,
            device_id=device, device_id_type=MESH)

    def send_q(r):
        p, s = peer(r), MIRROR[r]
        return remote(q_send.at[p], q_in.at[s], q_ss.at[r], q_rs.at[s], (blk, p))

    def send_kv(r):
        p, s = peer(r), MIRROR[r]
        return remote(kv_send.at[p], kv_in.at[s], kv_ss.at[r], kv_rs.at[s], (blk, p))

    def pass_kv(n):
        return remote(
            kv_in.at[pl.ds(4 * n, 4)], kv_in.at[pl.ds(8 + 4 * n, 4)],
            pass_ss.at[n], pass_rs.at[n], (before, head))

    def send_o(r):
        p = peer(r)
        return remote(o_send.at[r], o_in.at[head], o_ss.at[r], o_rs.at[head], (blk, p))

    left = lax.broadcasted_iota(jnp.int32, (HEAD_DIM, 128), 1) < HEAD_DIM
    half = TOK // 2

    def swap(x):
        return pltpu.roll(x, HEAD_DIM, 1)

    def transpose_into(src, dst, at):
        for pair in range(HEADS // 2):
            t = src[:, pair * 128:pair * 128 + 128].T
            dst[2 * pair, at:at + HEAD_DIM] = t[:HEAD_DIM]
            dst[2 * pair + 1, at:at + HEAD_DIM] = t[HEAD_DIM:]

    loads[0].wait()
    for pair in range(HEADS // 2):
        cols = slice(pair * 128, pair * 128 + 128)
        for c in range(4):
            a = k_ref[c * 64:c * 64 + 64, cols].astype(F32)
            b = k_ref[half + c * 64:half + c * 64 + 64, cols].astype(F32)
            lanes = slice(c * 128, c * 128 + 128)
            kv_send[2 * pair, 0:HEAD_DIM, lanes] = jnp.where(left, a, swap(b)).astype(BF16)
            kv_send[2 * pair + 1, 0:HEAD_DIM, lanes] = jnp.where(left, swap(a), b).astype(BF16)
    loads[1].wait()
    transpose_into(v_ref, kv_send, HEAD_DIM)
    pl.semaphore_wait(barrier, 8)
    for r in (1, 2, 3):
        send_kv(r).start()
    loads[2].wait()
    transpose_into(q_ref, q_send, 0)
    for r in range(1, 8):
        send_q(r).start()

    def widen_q(q, s):
        scaled = q.astype(F32) * SCALE
        high = scaled.astype(BF16)
        q_wide[s, 0:HEAD_DIM] = high
        q_wide[s, HEAD_DIM:2 * HEAD_DIM] = (scaled - high.astype(F32)).astype(BF16)

    def widen_kv(s):
        for c in range(4):
            x = kv_in[s, 0:HEAD_DIM, c * 128:c * 128 + 128].astype(F32)
            y = swap(x)
            k_wide[s, c * 64:c * 64 + 64] = jnp.where(left, x, y).astype(BF16)
            k_wide[s, half + c * 64:half + c * 64 + 64] = jnp.where(left, y, x).astype(BF16)
        v_wide[s, 0:HEAD_DIM] = kv_in[s, HEAD_DIM:2 * HEAD_DIM]

    kv_in[0] = kv_send[head]
    for s in range(16):
        v_wide[s, HEAD_DIM:VROWS] = jnp.ones((VROWS - HEAD_DIM, TOK), BF16)
    acc[...] = jnp.zeros_like(acc)
    top[...] = jnp.full(top.shape, -1e30, F32)
    widen_q(q_send[head], 0)
    widen_kv(0)

    def arrive(n):
        fresh = [r for r in range(4 * n, 4 * n + 4) if r > 0]
        for r in fresh:
            send_kv(MIRROR[r]).wait_recv()
        pass_kv(n).start()
        for r in fresh:
            widen_kv(r)

    def arrive_next(n):
        pass_kv(n).wait_recv()
        for r in range(8 + 4 * n, 12 + 4 * n):
            widen_kv(r)

    arrive(0)

    def where(t):
        n = (t >= 8).astype(jnp.int32) + (t >= 15).astype(jnp.int32) + (t >= 22).astype(jnp.int32)
        i = jnp.where(t >= 29, 0, jnp.where(t >= 22, 29 - t, t - 7 * n))
        g = jnp.where(t >= 29, t - 28, n)
        return i, jnp.where(g == 1, 2, jnp.where(g == 2, 1, g))

    def tile(dst, t, src, t_src, new):
        i, g = where(t)
        q = q_wide[i]
        if src is not None:
            g_src = where(t_src)[1]
        most = mixed = None
        for u in range(TILE // SUB):
            rows = slice(u * SUB, (u + 1) * SUB)
            part = slice((u % 2) * SUB, (u % 2 + 1) * SUB)
            s = jnp.dot(k_wide[g * GROUP + u // 2, part], q, preferred_element_type=F32)
            dst[rows] = s
            m = jnp.max(s, axis=0, keepdims=True)
            most = m if most is None else jnp.maximum(most, m)
            if src is not None:
                probs = jnp.exp2(src[rows] - new).astype(BF16)
                d = jnp.dot(
                    v_wide[g_src * GROUP + u // 2, :, part], probs, preferred_element_type=F32)
                mixed = d if mixed is None else mixed + d
        return most, mixed

    def step(now, later, t, most):
        @pl.when(t < 7)
        def _():
            r = t + 1
            remote(q_send.at[r], q_in.at[r], q_ss.at[r], q_rs.at[r], (before, head)).wait_recv()
            widen_q(q_in[r], r)

        def at(when, act):
            @pl.when(t == when)
            def _():
                act()

        def rest():
            for r in SECOND:
                send_kv(r).start()

        def far_arrive():
            arrive(1)

        at(3, rest)
        at(7, lambda: arrive_next(0))
        at(12, far_arrive)
        at(21, lambda: arrive_next(1))

        i = where(t)[0]
        old = top[i]
        new = jnp.maximum(old, most)
        top[i] = new
        most, mixed = tile(later, jnp.minimum(t + 1, 31), now, t, new)
        acc[i] = acc[i] * jnp.exp2(old - new) + mixed

        @pl.when(t >= 22)
        def _():
            a = acc[i]
            o_send[i] = (a[0:HEAD_DIM] / a[HEAD_DIM:HEAD_DIM + 1]).astype(BF16)

        for r in range(1, 8):
            @pl.when(t == 29 - r)
            def _():
                send_o(r).start()

        return most

    most, _ = tile(s_even, jnp.int32(0), None, 0, None)

    def two(n, most):
        most = step(s_even, s_odd, 2 * n, most)
        return step(s_odd, s_even, 2 * n + 1, most)

    lax.fori_loop(0, 16, two, most)

    o_in[head] = o_send[0]
    loads[3].wait()
    for r in range(1, 8):
        p = peer(r)
        remote(o_send.at[r], o_in.at[p], o_ss.at[r], o_rs.at[p], (blk, p)).wait_recv()
    mixed = o_in[...].reshape(WIDE, TOK)
    out_ref[...] = lax.dot_general(
        mixed, w_ref[...], (((0,), (0,)), ((), ())), preferred_element_type=F32
    ).astype(BF16)

    for r in range(1, 8):
        send_q(r).wait_send()
        send_kv(r).wait_send()
        send_o(r).wait_send()
    for n in range(2):
        pass_kv(n).wait_send()


def on_device(queries, keys, values, w_out):
    vmem = pl.BlockSpec(memory_space=pltpu.VMEM)
    hbm = pl.BlockSpec(memory_space=pltpu.HBM)
    dma = pltpu.SemaphoreType.DMA
    return pl.pallas_call(
        kernel,
        out_shape=jax.ShapeDtypeStruct((TOK, WIDE), BF16),
        in_specs=[hbm] * 4,
        out_specs=vmem,
        scratch_shapes=[
            *[pltpu.VMEM((TOK, WIDE), BF16)] * 4,
            dma((4,)),
            pltpu.VMEM((8, 2 * HEAD_DIM, TOK), BF16),
            pltpu.VMEM((8, HEAD_DIM, TOK), BF16),
            pltpu.VMEM((16, 2 * HEAD_DIM, TOK), BF16),
            pltpu.VMEM((8, HEAD_DIM, TOK), BF16),
            pltpu.VMEM((8, 2 * HEAD_DIM, TOK), BF16),
            pltpu.VMEM((16, TOK, 2 * HEAD_DIM), BF16),
            pltpu.VMEM((16, VROWS, TOK), BF16),
            pltpu.VMEM((8, VROWS, TOK), F32),
            pltpu.VMEM((8, 1, TOK), F32),
            pltpu.VMEM((TILE, TOK), F32),
            pltpu.VMEM((TILE, TOK), F32),
            pltpu.VMEM((8, HEAD_DIM, TOK), BF16),
            pltpu.VMEM((8, HEAD_DIM, TOK), BF16),
            dma((8,)), dma((8,)), dma((8,)), dma((8,)),
            dma((2,)), dma((2,)), dma((8,)), dma((8,)),
        ],
        compiler_params=pltpu.CompilerParams(
            collective_id=0, has_side_effects=True, vmem_limit_bytes=48 * 2**20
        ),
        cost_estimate=pl.CostEstimate(
            flops=2 * 2 * TOK * WIDE * 16 * TOK + 2 * TOK * WIDE * WIDE,
            bytes_accessed=5 * TOK * WIDE * 2,
            transcendentals=TOK * HEADS * 16 * TOK,
        ),
    )(queries, keys, values, w_out)


def solution(mesh):
    split = P(("blk", "head"), None)
    return jax.shard_map(
        on_device, mesh=mesh, in_specs=(split, split, split, P()), out_specs=split, check_vma=False
    )
```
